32 devices in a mesh: group: 2 (over y), store: 4 (over x, core), head: 4 (over z).
Axes of the slice: x: 2, y: 2, z: 4, core: 2. Of those that a mesh axis runs over, the one named last changes fastest.
Arguments:
- saved: bfloat16 [192, 64, 5120], P(('group', 'store'), None, 'head'), parts along dimension 0, may hold values from -6 to 6
- fresh: bfloat16 [8, 256, 5120], P(('group', 'store')), parts along dimension 0, may hold values from -6 to 6
- w_query: bfloat16 [5120, 2048], P(None, 'head'), may hold values from -0.078125 to 0.078125
- w_key: bfloat16 [5120, 512], P(None, 'head'), may hold values from -0.078125 to 0.078125
- w_value: bfloat16 [5120, 512], P(None, 'head'), may hold values from -0.078125 to 0.078125
- q_gain: float32 [128], replicated, may hold values from 0.8 to 2
- k_gain: float32 [128], replicated, may hold values from 0.8 to 2
- lengths: int32 [8], P('group'), parts along dimension 0, may hold values from 1 to 64, 96 in all
- slot_page: int32 [192], P(('group', 'store')), parts along dimension 0, may hold values from 0 to 95, each once
Outputs:
- attended: bfloat16 [8, 256, 2048], P(('group', 'store'), None, 'head'), parts along dimension 0
The draws below stay inside these ranges and needn't reach their ends.
There are 2 independent parts, one for each index of `group`. The reference program is written for one: setup_inputs(seed, part) draws one part's arguments, and reference() takes and returns one part's arrays. A program takes and returns all parts, laid end to end along the dimension named above; an argument that names none is the same for every part. Nothing has to cross between parts.
Inputs may be any that keep to these rules, and one draw needn't show every extreme that they name: The lengths of one group's sessions add up to 96, and the longest is exactly 64. Each value appears once in one group's slot_page.
All inputs are finite; a program needn't handle non-finite values.
Results may differ from the reference program's by a relative error of at most 0.0093.
Values may be sent and summed in bfloat16 or wider, within the bound.
A program may use at most 128 MiB of HBM per device.

```python
import math
import jax
import jax.numpy as jnp
import numpy as np
from jax import lax

D = 5120
HD = 128
QH_DEV = 4
PAGE = 64
NEW = 256
KVH = 4
QHEADS = 16
SESS = 4
TOTAL_PAGES = 96
MOST_PAGES = 64
N_HEAD = 4


def steps_of(stream_key, extent, cuts, least, high):
    def one(axis_at, shards_of):
        steps = jax.random.uniform(jax.random.fold_in(jax.random.fold_in(stream_key, 6), axis_at), (shards_of,), jnp.float32, least / len(cuts), high / len(cuts))
        return jnp.repeat(jnp.exp(steps), extent[axis_at] // shards_of).reshape((-1,) + (1,) * (len(extent) - axis_at - 1))

    level = one(*cuts[0])
    for cut in cuts[1:]:
        level = level * one(*cut)
    return level


def split_up(count, total, limit, lean):
    loads = [(1 << 20) // math.isqrt(standing ** lean) + 1 for standing in range(2, count + 1)]
    rest, holding = total - limit - (count - 1), [1] * (count - 1)
    while rest > 0:
        candidates = [i for i in range(count - 1) if holding[i] < limit]
        pool, remaining = sum([loads[i] for i in candidates]), rest
        for i in candidates:
            more = min(limit - holding[i], max(1, remaining * loads[i] // pool), rest)
            holding[i] = holding[i] + more
            rest = rest - more
    return np.array([limit] + holding)


def uneven_parts(rng, count, total, reach, lean):
    if count == 2:
        one = jax.random.randint(rng, (), max(1, total - reach), min(reach, total - 1) + 1)
        return jnp.stack([one, total - one])
    tallies = jnp.asarray(split_up(count, total, reach, lean), jnp.int32)
    pairs = (count - 1) // 2
    source_of, sink = tallies[1:1 + 2 * pairs:2], tallies[2:2 + 2 * pairs:2]
    margin = jnp.minimum(source_of - 1, reach - sink)
    moved = jax.random.randint(jax.random.fold_in(rng, 1), (pairs,), 0, 1 << 20) % (margin + 1)
    tallies = tallies.at[1:1 + 2 * pairs:2].set(source_of - moved).at[2:2 + 2 * pairs:2].set(sink + moved)
    return tallies[jax.random.permutation(jax.random.fold_in(rng, 2), count)]


def gaussian(rng, extent, spread, bound, pieces=(), kind=jnp.bfloat16):
    loudness = steps_of(rng, extent, pieces, -0.22, 0.18) if pieces else 1.0
    drawn = jax.random.normal(rng, extent, jnp.float32) * spread * loudness
    return jnp.minimum(jnp.maximum(drawn, -bound), bound).astype(kind)


def setup_inputs(seed: int = 0, part: int = 0) -> dict:
    key_of = jax.random.split(jax.random.key(seed), 10)
    part_keys = jax.random.split(jax.random.fold_in(key_of[9], part), 10)
    return {
        "saved": gaussian(part_keys[0], (TOTAL_PAGES, PAGE, D), 1.0, 6.0, ((0, 4), (2, 4))),
        "fresh": gaussian(part_keys[1], (SESS, NEW, D), 1.0, 6.0, ((0, 4),)),
        "w_query": gaussian(key_of[2], (D, QHEADS * HD), D ** -0.5, 0.078125, ((1, 4),)),
        "w_key": gaussian(key_of[3], (D, KVH * HD), D ** -0.5, 0.078125, ((1, 4),)),
        "w_value": gaussian(key_of[4], (D, KVH * HD), D ** -0.5, 0.078125, ((1, 4),)),
        "q_gain": jnp.clip(jnp.exp(jax.random.uniform(key_of[5], (HD,), jnp.float32, math.log(0.8), math.log(2.0))), 0.8, 2.0),
        "k_gain": jnp.clip(jnp.exp(jax.random.uniform(key_of[6], (HD,), jnp.float32, math.log(0.8), math.log(2.0))), 0.8, 2.0),
        "lengths": uneven_parts(part_keys[7], SESS, TOTAL_PAGES, MOST_PAGES, 2).astype(jnp.int32),
        "slot_page": jax.random.permutation(part_keys[8], TOTAL_PAGES).astype(jnp.int32),
    }


epsilon = 1e-06
rope_base = 1000000.0

def head_norm(values, gain):
    mean_sq = lax.optimization_barrier(jnp.mean(values * values, axis=-1, keepdims=True))
    return values * lax.rsqrt(mean_sq + epsilon) * gain

def rotary(values, positions):
    width = values.shape[-1]
    half_width = width // 2
    expo = jnp.arange(half_width, dtype=jnp.float32) * (2.0 / width)
    freqs = jnp.exp(-expo * math.log(rope_base))
    angles = positions.astype(jnp.float32)[:, None] * freqs[None, :]
    cosine = jnp.cos(angles)[:, None, :]
    sine = jnp.sin(angles)[:, None, :]
    first = values[..., :half_width]
    second = values[..., half_width:]
    return jnp.concatenate([first * cosine - second * sine, second * cosine + first * sine], axis=-1)

def reference(saved, fresh, w_query, w_key, w_value, q_gain, k_gain, lengths, slot_page):
    ends = jnp.cumsum(lengths).astype(jnp.int32)
    starts = ends - lengths
    session_of = lax.optimization_barrier(jnp.sum((slot_page[:, None] >= ends[None, :]).astype(jnp.int32), axis=1)).astype(jnp.int32)
    first_page = jnp.take(starts, session_of)
    key_pos = ((slot_page - first_page) * PAGE)[:, None] + jnp.arange(PAGE, dtype=jnp.int32)[None, :]
    new_pos = (lengths * PAGE)[:, None] + jnp.arange(NEW, dtype=jnp.int32)[None, :]
    saved_rows = saved.reshape(TOTAL_PAGES * PAGE, D)
    key_raw = jnp.dot(saved_rows, w_key, preferred_element_type=jnp.float32).reshape(-1, N_HEAD, HD)
    keys = rotary(head_norm(key_raw, k_gain), key_pos.reshape(-1)).astype(jnp.bfloat16)
    keys = keys.reshape(TOTAL_PAGES, PAGE, N_HEAD, HD)
    values = jnp.dot(saved_rows, w_value, preferred_element_type=jnp.float32).astype(jnp.bfloat16)
    values = values.reshape(TOTAL_PAGES, PAGE, N_HEAD, HD)
    turn_rows = fresh.reshape(SESS * NEW, D)
    query_raw = jnp.dot(turn_rows, w_query, preferred_element_type=jnp.float32).reshape(-1, N_HEAD * QH_DEV, HD)
    queries = rotary(head_norm(query_raw, q_gain), new_pos.reshape(-1)).astype(jnp.bfloat16)
    queries = queries.reshape(SESS, NEW, N_HEAD, QH_DEV, HD)
    new_raw = jnp.dot(turn_rows, w_key, preferred_element_type=jnp.float32).reshape(-1, N_HEAD, HD)
    new_keys = rotary(head_norm(new_raw, k_gain), new_pos.reshape(-1)).astype(jnp.bfloat16)
    new_keys = new_keys.reshape(SESS, NEW, N_HEAD, HD)
    new_values = jnp.dot(turn_rows, w_value, preferred_element_type=jnp.float32).astype(jnp.bfloat16)
    new_values = new_values.reshape(SESS, NEW, N_HEAD, HD)
    scale = math.sqrt(HD)

    def visit(carry, inputs):
        numer, denom = carry
        page_keys, page_values, session = inputs
        query_block = lax.dynamic_index_in_dim(queries, session, 0, keepdims=False).astype(jnp.float32)
        scores = jnp.einsum('qgjd,kgd->qgjk', query_block, page_keys.astype(jnp.float32)) / scale
        weight = jnp.exp(scores)
        weight_b = weight.astype(jnp.bfloat16).astype(jnp.float32)
        numer_add = jnp.einsum('qgjk,kgd->qgjd', weight_b, page_values.astype(jnp.float32))
        numer = numer.at[session].add(numer_add)
        denom = denom.at[session].add(lax.optimization_barrier(jnp.sum(weight, axis=-1)))
        return ((numer, denom), None)
    numer0 = jnp.zeros((SESS, NEW, N_HEAD, QH_DEV, HD), jnp.float32)
    denom0 = jnp.zeros((SESS, NEW, N_HEAD, QH_DEV), jnp.float32)
    (numer, denom), unused = lax.scan(visit, (numer0, denom0), (keys, values, session_of))
    own_scores = jnp.einsum('sqgjd,skgd->sqgjk', queries.astype(jnp.float32), new_keys.astype(jnp.float32)) / scale
    causal = jnp.arange(NEW)[None, :] <= jnp.arange(NEW)[:, None]
    own_weight = jnp.where(causal[None, :, None, None, :], jnp.exp(own_scores), jnp.float32(0.0))
    denom = denom + lax.optimization_barrier(jnp.sum(own_weight, axis=-1))
    own_b = own_weight.astype(jnp.bfloat16).astype(jnp.float32)
    numer = numer + jnp.einsum('sqgjk,skgd->sqgjd', own_b, new_values.astype(jnp.float32))
    attended = (numer / denom[..., None]).astype(jnp.bfloat16)
    return attended.reshape(SESS, NEW, N_HEAD * QH_DEV * HD)
```

```python
import math

import jax
import jax.numpy as jnp
from jax import lax
from jax.sharding import PartitionSpec as P

epsilon = 1e-06
rope_base = 1000000.0


def head_norm(values, gain):
    mean_sq = jnp.mean(values * values, axis=-1, keepdims=True)
    return values * lax.rsqrt(mean_sq + epsilon) * gain


def rotary(values, positions):
    width = values.shape[-1]
    half_width = width // 2
    expo = jnp.arange(half_width, dtype=jnp.float32) * (2.0 / width)
    freqs = jnp.exp(-expo * math.log(rope_base))
    angles = positions.astype(jnp.float32)[:, None] * freqs[None, :]
    cosine = jnp.cos(angles)[:, None, :]
    sine = jnp.sin(angles)[:, None, :]
    first = values[..., :half_width]
    second = values[..., half_width:]
    return jnp.concatenate(
        [first * cosine - second * sine, second * cosine + first * sine], axis=-1
    )


def shards(saved, fresh, w_query, w_key, w_value, q_gain, k_gain, lengths, slot_page):
    page_count, page_len, part_width = saved.shape
    head_dim = w_key.shape[1]
    w_pair = jnp.concatenate([w_key, w_value], axis=1)
    n_head = lax.axis_size("head")
    w_here = lax.all_to_all(
        w_pair.reshape(n_head, part_width, 2 * head_dim), "head", 0, 0, tiled=True
    )
    rows = saved.reshape(-1, part_width)
    partial = jnp.einsum(
        "rf,hfc->hrc", rows, w_here, preferred_element_type=jnp.float32
    ).astype(jnp.bfloat16)
    parts = lax.all_to_all(partial, "head", 0, 0, tiled=True)
    pair = jnp.sum(parts.astype(jnp.float32), axis=0)
    sess_count = lengths.shape[0]
    ends = jnp.cumsum(lengths)
    starts = ends - lengths
    session_of = jnp.sum((slot_page[:, None] >= ends[None, :]).astype(jnp.int32), axis=1)
    onehot = (session_of[:, None] == jnp.arange(sess_count, dtype=jnp.int32)[None, :]).astype(
        jnp.int32
    )
    first_page = jnp.sum(onehot * starts[None, :], axis=1)
    key_pos = ((slot_page - first_page) * page_len)[:, None] + jnp.arange(
        page_len, dtype=jnp.int32
    )[None, :]
    keys = rotary(head_norm(pair[:, None, :head_dim], k_gain), key_pos.reshape(-1)).astype(
        jnp.bfloat16
    )
    keys = keys.reshape(page_count, page_len, head_dim)
    values = pair[:, head_dim:].astype(jnp.bfloat16).reshape(page_count, page_len, head_dim)
    turn_rows = fresh[0]
    new_count = turn_rows.shape[0]
    group_heads = w_query.shape[1] // head_dim
    my_store = lax.axis_index("store")
    my_length = lax.dynamic_index_in_dim(lengths, my_store, 0, keepdims=False)
    new_pos = my_length * page_len + jnp.arange(new_count, dtype=jnp.int32)
    query_raw = jnp.dot(turn_rows, w_query, preferred_element_type=jnp.float32).reshape(
        new_count, group_heads, head_dim
    )
    queries = rotary(head_norm(query_raw, q_gain), new_pos).astype(jnp.bfloat16)
    new_raw = jnp.dot(turn_rows, w_key, preferred_element_type=jnp.float32)[:, None, :]
    new_keys = rotary(head_norm(new_raw, k_gain), new_pos).astype(jnp.bfloat16)[:, 0, :]
    new_values = jnp.dot(turn_rows, w_value, preferred_element_type=jnp.float32).astype(
        jnp.bfloat16
    )
    scale = math.sqrt(head_dim)
    every_query = lax.all_gather(queries[None], "store", axis=0, tiled=True)
    page_queries = jnp.take(every_query, session_of, axis=0)
    scores = (
        jnp.einsum("pqjd,pkd->pqjk", page_queries, keys, preferred_element_type=jnp.float32) / scale
    )
    weight = jnp.exp(scores)
    page_denom = jnp.sum(weight, axis=-1)
    page_numer = jnp.einsum(
        "pqjk,pkd->pqjd", weight.astype(jnp.bfloat16), values, preferred_element_type=jnp.float32
    )
    onehot_float = onehot.astype(jnp.float32)
    sess_numer = jnp.einsum(
        "ps,pqjd->sqjd", onehot_float, page_numer, precision=lax.Precision.HIGHEST
    )
    sess_denom = jnp.einsum(
        "ps,pqj->sqj", onehot_float, page_denom, precision=lax.Precision.HIGHEST
    )
    numer_all, denom_all = (
        lax.psum_scatter(sess_numer, "store", scatter_dimension=0, tiled=True),
        lax.psum_scatter(sess_denom, "store", scatter_dimension=0, tiled=True),
    )
    numer_in = numer_all[0]
    denom_in = denom_all[0]
    own_scores = (
        jnp.einsum("qjd,kd->qjk", queries, new_keys, preferred_element_type=jnp.float32) / scale
    )
    causal = jnp.arange(new_count)[None, :] <= jnp.arange(new_count)[:, None]
    own_weight = jnp.where(causal[:, None, :], jnp.exp(own_scores), jnp.float32(0.0))
    denom = denom_in + jnp.sum(own_weight, axis=-1)
    numer = numer_in + jnp.einsum(
        "qjk,kd->qjd",
        own_weight.astype(jnp.bfloat16),
        new_values,
        preferred_element_type=jnp.float32,
    )
    attended = (numer / denom[..., None]).astype(jnp.bfloat16)
    return attended.reshape(1, new_count, group_heads * head_dim)


def solution(mesh):
    return jax.shard_map(
        shards,
        mesh=mesh,
        in_specs=(
            P(("group", "store"), None, "head"),
            P(("group", "store"), None, None),
            P(None, "head"),
            P(None, "head"),
            P(None, "head"),
            P(),
            P(),
            P("group"),
            P(("group", "store")),
        ),
        out_specs=P(("group", "store"), None, "head"),
        check_vma=False,
    )
```

```python
import functools
import math

import jax
import jax.numpy as jnp
from jax import lax
from jax.experimental import pallas as pl
from jax.experimental.pallas import tpu as pltpu
from jax.sharding import PartitionSpec as P

epsilon = 1e-06
rope_base = 1000000.0
part_scale = 16.0


def head_norm(values, gain):
    mean_sq = jnp.mean(values * values, axis=-1, keepdims=True)
    return values * lax.rsqrt(mean_sq + epsilon) * gain


def rotary(values, positions):
    width = values.shape[-1]
    half_width = width // 2
    expo = jnp.arange(half_width, dtype=jnp.float32) * (2.0 / width)
    freqs = jnp.exp(-expo * math.log(rope_base))
    angles = positions.astype(jnp.float32)[:, None] * freqs[None, :]
    cosine = jnp.cos(angles)[:, None, :]
    sine = jnp.sin(angles)[:, None, :]
    first = values[..., :half_width]
    second = values[..., half_width:]
    return jnp.concatenate(
        [first * cosine - second * sine, second * cosine + first * sine], axis=-1
    )


def page_kernel(scale, session_ref, q_ref, k_ref, v_ref, numer_ref, denom_ref, numer, denom):
    pages = k_ref.shape[0]
    page_len = k_ref.shape[1]
    numer[...] = jnp.zeros_like(numer)
    denom[...] = jnp.zeros_like(denom)

    def body(p, carry):
        s = session_ref[p]
        scores = jnp.dot(k_ref[p], q_ref[s], preferred_element_type=jnp.float32)
        weight = jnp.exp(scores * scale)
        denom[s] += jnp.sum(weight.reshape(page_len // 8, 8, weight.shape[-1]), axis=0)
        numer[s] += lax.dot_general(
            v_ref[p],
            weight.astype(jnp.bfloat16),
            (((0,), (0,)), ((), ())),
            preferred_element_type=jnp.float32,
        )
        return carry

    lax.fori_loop(0, pages, body, 0, unroll=2)
    numer_ref[...] = numer[...].astype(jnp.bfloat16)
    denom_ref[...] = denom[...]


def page_attention(session_of, queries, keys, values, scale):
    sess_count, head_dim, columns = queries.shape
    return pl.pallas_call(
        functools.partial(page_kernel, scale),
        out_shape=(
            jax.ShapeDtypeStruct((sess_count, head_dim, columns), jnp.bfloat16),
            jax.ShapeDtypeStruct((sess_count, 8, columns), jnp.float32),
        ),
        in_specs=[pl.BlockSpec(memory_space=pltpu.SMEM)]
        + [pl.BlockSpec(memory_space=pltpu.VMEM)] * 3,
        out_specs=[pl.BlockSpec(memory_space=pltpu.VMEM)] * 2,
        scratch_shapes=[
            pltpu.VMEM((sess_count, head_dim, columns), jnp.float32),
            pltpu.VMEM((sess_count, 8, columns), jnp.float32),
        ],
        compiler_params=pltpu.CompilerParams(vmem_limit_bytes=48 * 1024 * 1024),
        cost_estimate=pl.CostEstimate(
            flops=4 * keys.size * columns, bytes_accessed=6 << 20, transcendentals=0
        ),
    )(session_of, queries, keys, values)


def shards(saved, fresh, w_query, w_key, w_value, q_gain, k_gain, lengths, slot_page):
    page_count, page_len, part_width = saved.shape
    head_dim = w_key.shape[1]
    n_head = lax.axis_size("head")
    n_store = lax.axis_size("store")
    my_store = lax.axis_index("store")
    sess_count = lengths.shape[0]
    share = part_width // n_store

    def my_rows(w):
        cut = w.reshape(n_head, n_store, share, head_dim)
        return lax.dynamic_index_in_dim(cut, my_store, 1, keepdims=False)

    w_share = jnp.concatenate([my_rows(w_key), my_rows(w_value)], axis=2)
    w_share = lax.all_to_all(w_share, "head", 0, 0, tiled=True)
    w_here = lax.all_gather(w_share, "store", axis=1, tiled=True)
    rows = saved.reshape(-1, part_width)
    partial = (
        jnp.einsum("rf,hfc->hrc", rows, w_here, preferred_element_type=jnp.float32) * part_scale
    ).astype(jnp.float16)
    parts = lax.all_to_all(partial, "head", 0, 0, tiled=True)
    pair = jnp.sum(parts.astype(jnp.float32), axis=0) * (1.0 / part_scale)

    ends = jnp.cumsum(lengths)
    starts = ends - lengths
    session_of = jnp.sum((slot_page[:, None] >= ends[None, :]).astype(jnp.int32), axis=1)
    onehot = (session_of[:, None] == jnp.arange(sess_count, dtype=jnp.int32)[None, :]).astype(
        jnp.int32
    )
    first_page = jnp.sum(onehot * starts[None, :], axis=1)
    key_pos = ((slot_page - first_page) * page_len)[:, None] + jnp.arange(
        page_len, dtype=jnp.int32
    )[None, :]
    keys = rotary(head_norm(pair[:, None, :head_dim], k_gain), key_pos.reshape(-1)).astype(
        jnp.bfloat16
    )
    keys = keys.reshape(page_count, page_len, head_dim)
    values = pair[:, head_dim:].astype(jnp.bfloat16).reshape(page_count, page_len, head_dim)

    turn_rows = fresh[0]
    new_count = turn_rows.shape[0]
    group_heads = w_query.shape[1] // head_dim
    my_length = lax.dynamic_index_in_dim(lengths, my_store, 0, keepdims=False)
    new_pos = my_length * page_len + jnp.arange(new_count, dtype=jnp.int32)
    query_raw = jnp.dot(turn_rows, w_query, preferred_element_type=jnp.float32).reshape(
        new_count, group_heads, head_dim
    )
    queries = rotary(head_norm(query_raw, q_gain), new_pos).astype(jnp.bfloat16)
    new_raw = jnp.dot(turn_rows, w_key, preferred_element_type=jnp.float32)[:, None, :]
    new_keys = rotary(head_norm(new_raw, k_gain), new_pos).astype(jnp.bfloat16)[:, 0, :]
    new_values = jnp.dot(turn_rows, w_value, preferred_element_type=jnp.float32).astype(
        jnp.bfloat16
    )
    scale = 1.0 / math.sqrt(head_dim)
    columns = group_heads * new_count
    q_t = queries.transpose(2, 1, 0).reshape(head_dim, columns)
    every_query = lax.all_gather(q_t, "store", axis=0)

    numer_t, denom_8 = page_attention(session_of, every_query, keys, values, scale)
    denom = jnp.sum(denom_8, axis=1)
    high = denom.astype(jnp.bfloat16)
    low = (denom - high.astype(jnp.float32)).astype(jnp.bfloat16)
    sent = jnp.concatenate([numer_t, high[:, None, :], low[:, None, :]], axis=1)
    got = lax.all_to_all(sent, "store", 0, 0, tiled=True)
    total = jnp.sum(got.astype(jnp.float32), axis=0)

    own_scores = jnp.dot(new_keys, q_t, preferred_element_type=jnp.float32) * scale
    token = jnp.arange(columns, dtype=jnp.int32) % new_count
    causal = jnp.arange(new_count)[:, None] <= token[None, :]
    own_weight = jnp.where(causal, jnp.exp(own_scores), jnp.float32(0.0))
    own_denom = jnp.sum(own_weight, axis=0)
    own_numer = jnp.einsum(
        "kd,kc->dc", new_values, own_weight.astype(jnp.bfloat16), preferred_element_type=jnp.float32
    )
    numer = total[:head_dim] + own_numer
    denom = total[head_dim] + total[head_dim + 1] + own_denom
    attended = (numer / denom[None, :]).astype(jnp.bfloat16)
    attended = attended.reshape(head_dim, group_heads, new_count).transpose(2, 1, 0)
    return attended.reshape(1, new_count, group_heads * head_dim)


def solution(mesh):
    return jax.shard_map(
        shards,
        mesh=mesh,
        in_specs=(
            P(("group", "store"), None, "head"),
            P(("group", "store"), None, None),
            P(None, "head"),
            P(None, "head"),
            P(None, "head"),
            P(),
            P(),
            P("group"),
            P(("group", "store")),
        ),
        out_specs=P(("group", "store"), None, "head"),
        check_vma=False,
    )
```

```python
import functools
import math

import jax
import jax.numpy as jnp
from jax import lax
from jax.experimental import pallas as pl
from jax.experimental.pallas import tpu as pltpu
from jax.sharding import PartitionSpec as P

epsilon = 1e-06
rope_base = 1000000.0
part_scale = 16.0


def head_norm(values, gain):
    mean_sq = jnp.mean(values * values, axis=-1, keepdims=True)
    return values * lax.rsqrt(mean_sq + epsilon) * gain


def rotary(values, positions):
    width = values.shape[-1]
    half_width = width // 2
    expo = jnp.arange(half_width, dtype=jnp.float32) * (2.0 / width)
    freqs = jnp.exp(-expo * math.log(rope_base))
    angles = positions.astype(jnp.float32)[:, None] * freqs[None, :]
    cosine = jnp.cos(angles)[:, None, :]
    sine = jnp.sin(angles)[:, None, :]
    first = values[..., :half_width]
    second = values[..., half_width:]
    return jnp.concatenate(
        [first * cosine - second * sine, second * cosine + first * sine], axis=-1
    )


MESH = pl.DeviceIdType.MESH


def weight_kernel(n_head, share_ref, own_ref, out_ref, own_sem, send_sem, z_sem, x_sem, c_sem, d_sem):
    group = lax.axis_index("group")
    store = lax.axis_index("store")
    head = lax.axis_index("head")
    quarter = lax.rem(store, 4)
    x_quarter = lax.rem(quarter + 2, 4)
    x_mate = (group, store - quarter + x_quarter, head)
    c_mate = (group, store + 1 - 2 * lax.rem(store, 2), head)

    def head_peer(o):
        return (group, store, lax.rem(head + o, n_head))

    barrier = pltpu.get_barrier_semaphore()
    for peer in [head_peer(o) for o in range(1, n_head)] + [x_mate, c_mate]:
        pl.semaphore_signal(barrier, inc=1, device_id=peer, device_id_type=MESH)
    own = pltpu.make_async_copy(own_ref, out_ref.at[head], own_sem)
    own.start()
    pl.semaphore_wait(barrier, n_head + 1)

    sends = []

    def send(src, dst, sem, kind, o, peer):
        copy = pltpu.make_async_remote_copy(
            src_ref=src,
            dst_ref=dst,
            send_sem=send_sem.at[kind, o - 1],
            recv_sem=sem.at[o - 1],
            device_id=peer,
            device_id_type=MESH,
        )
        copy.start()
        sends.append(copy)
        return copy

    first, second, third, fourth = {}, {}, {}, {}
    for o in range(1, n_head):
        target = lax.rem(head + o, n_head)
        first[o] = send(
            share_ref.at[target], out_ref.at[head, quarter], z_sem, 0, o, head_peer(o)
        )
    for o in range(1, n_head):
        source = lax.rem(head + n_head - o, n_head)
        first[o].wait_recv()
        slot = out_ref.at[source, quarter]
        second[o] = send(slot, slot, x_sem, 1, o, x_mate)
        third[o] = send(slot, slot, c_sem, 2, o, c_mate)
    for o in range(1, n_head):
        source = lax.rem(head + n_head - o, n_head)
        second[o].wait_recv()
        slot = out_ref.at[source, x_quarter]
        fourth[o] = send(slot, slot, d_sem, 3, o, c_mate)
    for o in range(1, n_head):
        third[o].wait_recv()
        fourth[o].wait_recv()
    for copy in sends:
        copy.wait_send()
    own.wait()


def gather_weights(share, own):
    n_head = share.shape[0]
    return pl.pallas_call(
        functools.partial(weight_kernel, n_head),
        out_shape=jax.ShapeDtypeStruct((n_head,) + own.shape, share.dtype),
        in_specs=[pl.BlockSpec(memory_space=pl.ANY)] * 2,
        out_specs=pl.BlockSpec(memory_space=pl.ANY),
        scratch_shapes=[
            pltpu.SemaphoreType.DMA,
            pltpu.SemaphoreType.DMA((4, n_head - 1)),
            pltpu.SemaphoreType.DMA((n_head - 1,)),
            pltpu.SemaphoreType.DMA((n_head - 1,)),
            pltpu.SemaphoreType.DMA((n_head - 1,)),
            pltpu.SemaphoreType.DMA((n_head - 1,)),
        ],
        compiler_params=pltpu.CompilerParams(collective_id=0, has_side_effects=True),
        cost_estimate=pl.CostEstimate(flops=0, bytes_accessed=4 << 20, transcendentals=0),
    )(share, own)


def page_kernel(
    scale, n_block, session_ref, q_ref, gain_ref, cos_ref, sin_ref, *refs
):
    pair_refs = refs[:n_block]
    numer_ref, denom_ref, numer, denom = refs[n_block:]
    page_len, head_dim = cos_ref.shape[1:]
    numer[...] = jnp.zeros_like(numer)
    denom[...] = jnp.zeros_like(denom)
    gain = gain_ref[...]

    for block, pair_ref in enumerate(pair_refs):
        pages = pair_ref.shape[0]

        def body(i, carry):
            p = block * pages + i
            s = session_ref[p]
            raw = pair_ref[i, :, :head_dim]
            mean_sq = jnp.mean(raw * raw, axis=-1, keepdims=True)
            normed = raw * lax.rsqrt(mean_sq + epsilon) * gain
            turned = pltpu.roll(normed, head_dim // 2, 1)
            keys = (normed * cos_ref[p] + turned * sin_ref[p]).astype(jnp.bfloat16)
            values = pair_ref[i, :, head_dim:].astype(jnp.bfloat16)
            scores = jnp.dot(keys, q_ref[s], preferred_element_type=jnp.float32)
            weight = jnp.exp(scores * scale)
            denom[s] += jnp.sum(weight.reshape(page_len // 8, 8, weight.shape[-1]), axis=0)
            numer[s] += lax.dot_general(
                values,
                weight.astype(jnp.bfloat16),
                (((0,), (0,)), ((), ())),
                preferred_element_type=jnp.float32,
            )
            return carry

        lax.fori_loop(0, pages, body, 0, unroll=2)
    numer_ref[...] = numer[...].astype(jnp.bfloat16)
    denom_ref[...] = denom[...]


def page_attention(session_of, queries, gain, cosine, sine, pairs, scale):
    sess_count, head_dim, columns = queries.shape
    return pl.pallas_call(
        functools.partial(page_kernel, scale, len(pairs)),
        out_shape=(
            jax.ShapeDtypeStruct((sess_count, head_dim, columns), jnp.bfloat16),
            jax.ShapeDtypeStruct((sess_count, 8, columns), jnp.float32),
        ),
        in_specs=[pl.BlockSpec(memory_space=pltpu.SMEM)]
        + [pl.BlockSpec(memory_space=pltpu.VMEM)] * (4 + len(pairs)),
        out_specs=[pl.BlockSpec(memory_space=pltpu.VMEM)] * 2,
        scratch_shapes=[
            pltpu.VMEM((sess_count, head_dim, columns), jnp.float32),
            pltpu.VMEM((sess_count, 8, columns), jnp.float32),
        ],
        compiler_params=pltpu.CompilerParams(vmem_limit_bytes=48 * 1024 * 1024),
        cost_estimate=pl.CostEstimate(
            flops=4 * cosine.size * columns, bytes_accessed=6 << 20, transcendentals=0
        ),
    )(session_of, queries, gain[None, :], cosine, sine, *pairs)


def shards(saved, fresh, w_query, w_key, w_value, q_gain, k_gain, lengths, slot_page):
    page_count, page_len, part_width = saved.shape
    head_dim = w_key.shape[1]
    n_head = lax.axis_size("head")
    n_store = lax.axis_size("store")
    my_store = lax.axis_index("store")
    sess_count = lengths.shape[0]
    head = lax.axis_index("head")
    w_pair = jnp.concatenate([w_key, w_value], axis=1).reshape(
        n_head, 4, part_width // 4, 2 * head_dim
    )
    w_share = lax.dynamic_index_in_dim(w_pair, lax.rem(my_store, 4), 1, keepdims=False)
    w_own = lax.dynamic_index_in_dim(w_pair, head, 0, keepdims=False)
    w_here = gather_weights(w_share, w_own).reshape(n_head, part_width, 2 * head_dim)

    n_block = 2 if page_count % 2 == 0 else 1
    block_pages = page_count // n_block
    blocks = [
        saved[i * block_pages : (i + 1) * block_pages].reshape(-1, part_width)
        for i in range(n_block)
    ]

    def product(block, target):
        weights = lax.dynamic_index_in_dim(w_here, target, 0, keepdims=False)
        return jnp.dot(block, weights, preferred_element_type=jnp.float32) * part_scale

    ups = [None] * n_block
    downs = [None] * n_block
    for r in range(n_head - 1):
        up_to = jnp.minimum(n_head - 1 - r + head, n_head - 1)
        down_to = jnp.maximum(r - (n_head - 1) + head, 0)
        up_pairs = [(i, i + 1) for i in range(r + 1)]
        down_pairs = [(n_head - 1 - i, n_head - 2 - i) for i in range(r + 1)]
        for i, block in enumerate(blocks):
            up = product(block, up_to)
            down = product(block, down_to)
            if r > 0:
                up = up + ups[i].astype(jnp.float32)
                down = down + downs[i].astype(jnp.float32)
            ups[i] = lax.ppermute(up.astype(jnp.float16), "head", up_pairs)
            downs[i] = lax.ppermute(down.astype(jnp.float16), "head", down_pairs)
    pairs = []
    for i, block in enumerate(blocks):
        total = product(block, head) + (
            ups[i].astype(jnp.float32) + downs[i].astype(jnp.float32)
        )
        pairs.append((total * (1.0 / part_scale)).reshape(block_pages, page_len, 2 * head_dim))

    ends = jnp.cumsum(lengths)
    starts = ends - lengths
    session_of = jnp.sum((slot_page[:, None] >= ends[None, :]).astype(jnp.int32), axis=1)
    onehot = (session_of[:, None] == jnp.arange(sess_count, dtype=jnp.int32)[None, :]).astype(
        jnp.int32
    )
    first_page = jnp.sum(onehot * starts[None, :], axis=1)
    key_pos = ((slot_page - first_page) * page_len)[:, None] + jnp.arange(
        page_len, dtype=jnp.int32
    )[None, :]
    half = head_dim // 2
    freqs = jnp.exp(
        -jnp.arange(half, dtype=jnp.float32) * (2.0 / head_dim) * math.log(rope_base)
    )
    angles = key_pos.astype(jnp.float32)[:, :, None] * freqs[None, None, :]
    cosine, sine = jnp.cos(angles), jnp.sin(angles)
    cosine = jnp.concatenate([cosine, cosine], axis=-1)
    sine = jnp.concatenate([-sine, sine], axis=-1)

    turn_rows = fresh[0]
    new_count = turn_rows.shape[0]
    group_heads = w_query.shape[1] // head_dim
    my_length = lax.dynamic_index_in_dim(lengths, my_store, 0, keepdims=False)
    new_pos = my_length * page_len + jnp.arange(new_count, dtype=jnp.int32)
    query_raw = jnp.dot(turn_rows, w_query, preferred_element_type=jnp.float32).reshape(
        new_count, group_heads, head_dim
    )
    queries = rotary(head_norm(query_raw, q_gain), new_pos).astype(jnp.bfloat16)
    new_raw = jnp.dot(turn_rows, w_key, preferred_element_type=jnp.float32)[:, None, :]
    new_keys = rotary(head_norm(new_raw, k_gain), new_pos).astype(jnp.bfloat16)[:, 0, :]
    new_values = jnp.dot(turn_rows, w_value, preferred_element_type=jnp.float32).astype(
        jnp.bfloat16
    )
    scale = 1.0 / math.sqrt(head_dim)
    columns = group_heads * new_count
    q_t = queries.transpose(2, 1, 0).reshape(head_dim, columns)
    every_query = lax.all_gather(q_t, "store", axis=0)

    numer_t, denom_8 = page_attention(
        session_of, every_query, k_gain, cosine, sine, pairs, scale
    )
    denom = jnp.sum(denom_8, axis=1)
    high = denom.astype(jnp.bfloat16)
    low = (denom - high.astype(jnp.float32)).astype(jnp.bfloat16)
    sent = jnp.concatenate([numer_t, high[:, None, :], low[:, None, :]], axis=1)
    got = lax.all_to_all(sent, "store", 0, 0, tiled=True)
    total = jnp.sum(got.astype(jnp.float32), axis=0)

    own_scores = jnp.dot(new_keys, q_t, preferred_element_type=jnp.float32) * scale
    token = jnp.arange(columns, dtype=jnp.int32) % new_count
    causal = jnp.arange(new_count)[:, None] <= token[None, :]
    own_weight = jnp.where(causal, jnp.exp(own_scores), jnp.float32(0.0))
    own_denom = jnp.sum(own_weight, axis=0)
    own_numer = jnp.einsum(
        "kd,kc->dc", new_values, own_weight.astype(jnp.bfloat16), preferred_element_type=jnp.float32
    )
    numer = total[:head_dim] + own_numer
    denom = total[head_dim] + total[head_dim + 1] + own_denom
    attended = (numer / denom[None, :]).astype(jnp.bfloat16)
    attended = attended.reshape(head_dim, group_heads, new_count).transpose(2, 1, 0)
    return attended.reshape(1, new_count, group_heads * head_dim)


def solution(mesh):
    return jax.shard_map(
        shards,
        mesh=mesh,
        in_specs=(
            P(("group", "store"), None, "head"),
            P(("group", "store"), None, None),
            P(None, "head"),
            P(None, "head"),
            P(None, "head"),
            P(),
            P(),
            P("group"),
            P(("group", "store")),
        ),
        out_specs=P(("group", "store"), None, "head"),
        check_vma=False,
    )
```

```python
import functools
import math

import jax
import jax.numpy as jnp
from jax import lax
from jax.experimental import pallas as pl
from jax.experimental.pallas import tpu as pltpu
from jax.sharding import PartitionSpec as P

epsilon = 1e-06
rope_base = 1000000.0
part_scale = 16.0


MESH = pl.DeviceIdType.MESH


def weight_kernel(
    n_head,
    w_key,
    w_value,
    w_query,
    fresh,
    q_gain,
    k_gain,
    cos_ref,
    sin_ref,
    out_ref,
    query_ref,
    new_key_ref,
    new_value_ref,
    wq,
    wk,
    wv,
    rows,
    q_acc,
    k_acc,
    v_acc,
    own_sem,
    load_sem,
    send_sem,
    z_sem,
    x_sem,
    c_sem,
    d_sem,
):
    group = lax.axis_index("group")
    store = lax.axis_index("store")
    head = lax.axis_index("head")
    part = w_key.shape[0] // n_head
    share = part // 4
    head_dim = w_key.shape[1]
    quarter = lax.rem(store, 4)
    x_quarter = lax.rem(quarter + 2, 4)
    x_mate = (group, store - quarter + x_quarter, head)
    c_mate = (group, store + 1 - 2 * lax.rem(store, 2), head)

    def head_peer(o):
        return (group, store, lax.rem(head + o, n_head))

    barrier = pltpu.get_barrier_semaphore()
    for peer in [head_peer(o) for o in range(1, n_head)] + [x_mate, c_mate]:
        pl.semaphore_signal(barrier, inc=1, device_id=peer, device_id_type=MESH)
    pl.semaphore_wait(barrier, n_head + 1)

    sends = []

    def send(src, dst, send_at, recv_at, peer):
        copy = pltpu.make_async_remote_copy(
            src_ref=src,
            dst_ref=dst,
            send_sem=send_at,
            recv_sem=recv_at,
            device_id=peer,
            device_id_type=MESH,
        )
        copy.start()
        sends.append(copy)
        return copy

    def share_rows(base, at):
        return pl.ds(pl.multiple_of(base + at * share, 16), share)

    first, second, third, fourth = {}, {}, {}, {}
    for o in range(1, n_head):
        target = lax.rem(head + o, n_head)
        for side, w in enumerate((w_key, w_value)):
            first[o, side] = send(
                w.at[share_rows(target * part, quarter)],
                out_ref.at[head, share_rows(0, quarter), side * head_dim : (side + 1) * head_dim],
                send_sem.at[side, o - 1],
                z_sem.at[side, o - 1],
                head_peer(o),
            )
    local = []
    for at, (src, dst) in enumerate(((fresh, rows), (w_query, wq), (w_key, wk), (w_value, wv))):
        local.append(pltpu.make_async_copy(src, dst, load_sem.at[at]))
    for side, w in enumerate((w_key, w_value)):
        local.append(
            pltpu.make_async_copy(
                w.at[pl.ds(pl.multiple_of(head * part, 16), part)],
                out_ref.at[head, :, side * head_dim : (side + 1) * head_dim],
                own_sem.at[side],
            )
        )
    for copy in local:
        copy.start()
    for copy in local[:4]:
        copy.wait()

    def project(o):
        cut = slice(o * part, (o + 1) * part)
        left = rows[:, cut]
        for acc, w in ((q_acc, wq), (k_acc, wk), (v_acc, wv)):
            term = jnp.dot(left, w[cut, :], preferred_element_type=jnp.float32)
            if o == 0:
                acc[...] = term
            else:
                acc[...] += term

    project(0)
    for o in range(1, n_head):
        source = lax.rem(head + n_head - o, n_head)
        first[o, 0].wait_recv()
        first[o, 1].wait_recv()
        slot = out_ref.at[source, share_rows(0, quarter)]
        second[o] = send(slot, slot, send_sem.at[2, o - 1], x_sem.at[o - 1], x_mate)
        third[o] = send(slot, slot, send_sem.at[3, o - 1], c_sem.at[o - 1], c_mate)
        project(o)
    for o in range(1, n_head):
        source = lax.rem(head + n_head - o, n_head)
        second[o].wait_recv()
        slot = out_ref.at[source, share_rows(0, x_quarter)]
        fourth[o] = send(slot, slot, send_sem.at[4, o - 1], d_sem.at[o - 1], c_mate)

    def turn(raw, gain):
        mean_sq = jnp.mean(raw * raw, axis=-1, keepdims=True)
        normed = raw * lax.rsqrt(mean_sq + epsilon) * gain
        turned = pltpu.roll(normed, head_dim // 2, 1)
        return (normed * cos_ref[...] + turned * sin_ref[...]).astype(jnp.bfloat16)

    for j in range(q_acc.shape[1] // head_dim):
        cut = slice(j * head_dim, (j + 1) * head_dim)
        query_ref[:, cut] = turn(q_acc[:, cut], q_gain[...])
    new_key_ref[...] = turn(k_acc[...], k_gain[...])
    new_value_ref[...] = v_acc[...].astype(jnp.bfloat16)

    for o in range(1, n_head):
        third[o].wait_recv()
        fourth[o].wait_recv()
    for copy in sends:
        copy.wait_send()
    for copy in local[4:]:
        copy.wait()


def gather_weights(n_head, w_key, w_value, w_query, rows, q_gain, k_gain, cosine, sine):
    features, head_dim = w_key.shape
    new_count = rows.shape[0]
    bf16, f32 = jnp.bfloat16, jnp.float32
    any_space = pl.BlockSpec(memory_space=pl.ANY)
    vmem = pl.BlockSpec(memory_space=pltpu.VMEM)
    dma = pltpu.SemaphoreType.DMA
    return pl.pallas_call(
        functools.partial(weight_kernel, n_head),
        out_shape=(
            jax.ShapeDtypeStruct((n_head, features // n_head, 2 * head_dim), bf16),
            jax.ShapeDtypeStruct((new_count, w_query.shape[1]), bf16),
            jax.ShapeDtypeStruct((new_count, head_dim), bf16),
            jax.ShapeDtypeStruct((new_count, head_dim), bf16),
        ),
        in_specs=[any_space] * 4 + [vmem] * 4,
        out_specs=[any_space] + [vmem] * 3,
        scratch_shapes=[
            pltpu.VMEM(w_query.shape, bf16),
            pltpu.VMEM(w_key.shape, bf16),
            pltpu.VMEM(w_value.shape, bf16),
            pltpu.VMEM(rows.shape, bf16),
            pltpu.VMEM((new_count, w_query.shape[1]), f32),
            pltpu.VMEM((new_count, head_dim), f32),
            pltpu.VMEM((new_count, head_dim), f32),
            dma((2,)),
            dma((4,)),
            dma((5, n_head - 1)),
            dma((2, n_head - 1)),
            dma((n_head - 1,)),
            dma((n_head - 1,)),
            dma((n_head - 1,)),
        ],
        compiler_params=pltpu.CompilerParams(
            collective_id=0, has_side_effects=True, vmem_limit_bytes=48 * 1024 * 1024
        ),
        cost_estimate=pl.CostEstimate(
            flops=2 * rows.size * 768, bytes_accessed=16 << 20, transcendentals=0
        ),
    )(w_key, w_value, w_query, rows, q_gain[None, :], k_gain[None, :], cosine, sine)


def page_kernel(
    scale, n_block, session_ref, q_ref, gain_ref, page_turn, row_turn, *refs
):
    pair_refs = refs[:n_block]
    numer_ref, denom_ref, numer, denom = refs[n_block:]
    page_len, head_dim = row_turn.shape[1:]
    numer[...] = jnp.zeros_like(numer)
    denom[...] = jnp.zeros_like(denom)
    gain = gain_ref[...]

    for block, pair_ref in enumerate(pair_refs):
        pages = pair_ref.shape[0] // page_len

        def body(i, carry):
            p = block * pages + i
            s = session_ref[p]
            here = pl.ds(pl.multiple_of(i * page_len, 8), page_len)
            raw = pair_ref[here, :head_dim]
            mean_sq = jnp.mean(raw * raw, axis=-1, keepdims=True)
            normed = raw * lax.rsqrt(mean_sq + epsilon) * gain
            turned = pltpu.roll(normed, head_dim // 2, 1)
            page_cos, page_sin = page_turn[p, 0:1, :], page_turn[p, 1:2, :]
            cosine = page_cos * row_turn[0] - page_sin * row_turn[1]
            sine = page_sin * row_turn[2] + page_cos * row_turn[3]
            keys = (normed * cosine + turned * sine).astype(jnp.bfloat16)
            values = pair_ref[here, head_dim:].astype(jnp.bfloat16)
            scores = jnp.dot(keys, q_ref[s], preferred_element_type=jnp.float32)
            weight = jnp.exp(scores * scale)
            denom[s] += jnp.sum(weight.reshape(page_len // 8, 8, weight.shape[-1]), axis=0)
            numer[s] += lax.dot_general(
                values,
                weight.astype(jnp.bfloat16),
                (((0,), (0,)), ((), ())),
                preferred_element_type=jnp.float32,
            )
            return carry

        lax.fori_loop(0, pages, body, 0, unroll=2)
    numer_ref[...] = numer[...].astype(jnp.bfloat16)
    denom_ref[...] = denom[...]


def page_attention(session_of, queries, gain, page_turn, row_turn, pairs, scale):
    sess_count, head_dim, columns = queries.shape
    return pl.pallas_call(
        functools.partial(page_kernel, scale, len(pairs)),
        out_shape=(
            jax.ShapeDtypeStruct((sess_count, head_dim, columns), jnp.bfloat16),
            jax.ShapeDtypeStruct((sess_count, 8, columns), jnp.float32),
        ),
        in_specs=[pl.BlockSpec(memory_space=pltpu.SMEM)]
        + [pl.BlockSpec(memory_space=pltpu.VMEM)] * (4 + len(pairs)),
        out_specs=[pl.BlockSpec(memory_space=pltpu.VMEM)] * 2,
        scratch_shapes=[
            pltpu.VMEM((sess_count, head_dim, columns), jnp.float32),
            pltpu.VMEM((sess_count, 8, columns), jnp.float32),
        ],
        compiler_params=pltpu.CompilerParams(vmem_limit_bytes=48 * 1024 * 1024),
        cost_estimate=pl.CostEstimate(
            flops=4 * pairs[0].size * len(pairs) * columns // 2, bytes_accessed=6 << 20, transcendentals=0
        ),
    )(session_of, queries, gain[None, :], page_turn, row_turn, *pairs)


def shards(saved, fresh, w_query, w_key, w_value, q_gain, k_gain, lengths, slot_page):
    page_count, page_len, part_width = saved.shape
    head_dim = w_key.shape[1]
    n_head = lax.axis_size("head")
    n_store = lax.axis_size("store")
    my_store = lax.axis_index("store")
    sess_count = lengths.shape[0]
    head = lax.axis_index("head")
    head = lax.axis_index("head")
    half = head_dim // 2
    freqs = jnp.exp(
        -jnp.arange(half, dtype=jnp.float32) * (2.0 / head_dim) * math.log(rope_base)
    )
    turn_rows = fresh[0]
    new_count = turn_rows.shape[0]
    group_heads = w_query.shape[1] // head_dim
    my_length = lax.dynamic_index_in_dim(lengths, my_store, 0, keepdims=False)
    new_pos = my_length * page_len + jnp.arange(new_count, dtype=jnp.int32)
    angles = new_pos.astype(jnp.float32)[:, None] * freqs[None, :]
    new_cos, new_sin = jnp.cos(angles), jnp.sin(angles)
    w_here, queries, new_keys, new_values = gather_weights(
        n_head,
        w_key,
        w_value,
        w_query,
        turn_rows,
        q_gain,
        k_gain,
        jnp.concatenate([new_cos, new_cos], axis=-1),
        jnp.concatenate([-new_sin, new_sin], axis=-1),
    )
    w_here, slot_page, lengths = lax.optimization_barrier((w_here, slot_page, lengths))

    n_block = 2 if page_count % 2 == 0 else 1
    block_pages = page_count // n_block
    products = [
        (
            jnp.einsum(
                "rf,hfc->hrc",
                saved[i * block_pages : (i + 1) * block_pages].reshape(-1, part_width),
                w_here,
                preferred_element_type=jnp.float32,
            )
            * part_scale
        ).astype(jnp.float16)
        for i in range(n_block)
    ]

    def product(block, target):
        return lax.dynamic_index_in_dim(block, target, 0, keepdims=False).astype(jnp.float32)

    ups = [None] * n_block
    downs = [None] * n_block
    for r in range(n_head - 1):
        up_to = jnp.minimum(n_head - 1 - r + head, n_head - 1)
        down_to = jnp.maximum(r - (n_head - 1) + head, 0)
        up_pairs = [(i, i + 1) for i in range(r + 1)]
        down_pairs = [(n_head - 1 - i, n_head - 2 - i) for i in range(r + 1)]
        for i, block in enumerate(products):
            up = product(block, up_to)
            down = product(block, down_to)
            if r > 0:
                up = up + ups[i].astype(jnp.float32)
                down = down + downs[i].astype(jnp.float32)
            ups[i] = lax.ppermute(up.astype(jnp.float16), "head", up_pairs)
            downs[i] = lax.ppermute(down.astype(jnp.float16), "head", down_pairs)
    pairs = []
    for i, block in enumerate(products):
        total = product(block, head) + (
            ups[i].astype(jnp.float32) + downs[i].astype(jnp.float32)
        )
        pairs.append(total * (1.0 / part_scale))

    ends = jnp.cumsum(lengths)
    starts = ends - lengths
    session_of = jnp.sum((slot_page[:, None] >= ends[None, :]).astype(jnp.int32), axis=1)
    onehot = (session_of[:, None] == jnp.arange(sess_count, dtype=jnp.int32)[None, :]).astype(
        jnp.int32
    )
    first_page = jnp.sum(onehot * starts[None, :], axis=1)
    page_pos = (slot_page - first_page) * page_len
    page_angle = page_pos.astype(jnp.float32)[:, None] * freqs[None, :]
    page_turn = jnp.stack([jnp.cos(page_angle), jnp.sin(page_angle)], axis=1)
    page_turn = jnp.concatenate([page_turn, page_turn], axis=-1)
    row_angle = jnp.arange(page_len, dtype=jnp.float32)[:, None] * freqs[None, :]
    cosine, sine = jnp.cos(row_angle), jnp.sin(row_angle)
    row_turn = jnp.stack(
        [
            jnp.concatenate([cosine, cosine], axis=-1),
            jnp.concatenate([sine, sine], axis=-1),
            jnp.concatenate([-cosine, cosine], axis=-1),
            jnp.concatenate([-sine, sine], axis=-1),
        ]
    )

    scale = 1.0 / math.sqrt(head_dim)
    columns = group_heads * new_count
    q_t = (
        queries.reshape(new_count, group_heads, head_dim)
        .transpose(2, 1, 0)
        .reshape(head_dim, columns)
    )
    every_query = lax.all_gather(q_t, "store", axis=0)

    numer_t, denom_8 = page_attention(
        session_of, every_query, k_gain, page_turn, row_turn, pairs, scale
    )
    denom = jnp.sum(denom_8, axis=1)
    high = denom.astype(jnp.bfloat16)
    low = (denom - high.astype(jnp.float32)).astype(jnp.bfloat16)
    sent = jnp.concatenate([numer_t, high[:, None, :], low[:, None, :]], axis=1)
    got = lax.all_to_all(sent, "store", 0, 0, tiled=True)
    total = jnp.sum(got.astype(jnp.float32), axis=0)

    own_scores = jnp.dot(new_keys, q_t, preferred_element_type=jnp.float32) * scale
    token = jnp.arange(columns, dtype=jnp.int32) % new_count
    causal = jnp.arange(new_count)[:, None] <= token[None, :]
    own_weight = jnp.where(causal, jnp.exp(own_scores), jnp.float32(0.0))
    own_denom = jnp.sum(own_weight, axis=0)
    own_numer = jnp.einsum(
        "kd,kc->dc", new_values, own_weight.astype(jnp.bfloat16), preferred_element_type=jnp.float32
    )
    numer = total[:head_dim] + own_numer
    denom = total[head_dim] + total[head_dim + 1] + own_denom
    attended = (numer / denom[None, :]).astype(jnp.bfloat16)
    attended = attended.reshape(head_dim, group_heads, new_count).transpose(2, 1, 0)
    return attended.reshape(1, new_count, group_heads * head_dim)


def solution(mesh):
    return jax.shard_map(
        shards,
        mesh=mesh,
        in_specs=(
            P(("group", "store"), None, "head"),
            P(("group", "store"), None, None),
            P(None, "head"),
            P(None, "head"),
            P(None, "head"),
            P(),
            P(),
            P("group"),
            P(("group", "store")),
        ),
        out_specs=P(("group", "store"), None, "head"),
        check_vma=False,
    )
```

```python
import functools
import math

import jax
import jax.numpy as jnp
from jax import lax
from jax.experimental import pallas as pl
from jax.experimental.pallas import tpu as pltpu
from jax.sharding import PartitionSpec as P

epsilon = 1e-06
rope_base = 1000000.0
part_scale = 16.0


MESH = pl.DeviceIdType.MESH


def weight_kernel(
    n_head,
    w_key,
    w_value,
    w_query,
    fresh,
    q_gain,
    k_gain,
    cos_ref,
    sin_ref,
    out_ref,
    query_ref,
    new_key_ref,
    new_value_ref,
    wq,
    wk,
    wv,
    rows,
    q_acc,
    k_acc,
    v_acc,
    own_sem,
    load_sem,
    send_sem,
    z_sem,
    x_sem,
    c_sem,
    d_sem,
):
    group = lax.axis_index("group")
    store = lax.axis_index("store")
    head = lax.axis_index("head")
    part = w_key.shape[0] // n_head
    share = part // 4
    head_dim = w_key.shape[1]
    quarter = lax.rem(store, 4)
    x_quarter = lax.rem(quarter + 2, 4)
    x_mate = (group, store - quarter + x_quarter, head)
    c_mate = (group, store + 1 - 2 * lax.rem(store, 2), head)

    def head_peer(o):
        return (group, store, lax.rem(head + o, n_head))

    barrier = pltpu.get_barrier_semaphore()
    for peer in [head_peer(o) for o in range(1, n_head)] + [x_mate, c_mate]:
        pl.semaphore_signal(barrier, inc=1, device_id=peer, device_id_type=MESH)
    pl.semaphore_wait(barrier, n_head + 1)

    sends = []

    def send(src, dst, send_at, recv_at, peer):
        copy = pltpu.make_async_remote_copy(
            src_ref=src,
            dst_ref=dst,
            send_sem=send_at,
            recv_sem=recv_at,
            device_id=peer,
            device_id_type=MESH,
        )
        copy.start()
        sends.append(copy)
        return copy

    def share_rows(base, at):
        return pl.ds(pl.multiple_of(base + at * share, 16), share)

    first, second, third, fourth = {}, {}, {}, {}
    for o in range(1, n_head):
        target = lax.rem(head + o, n_head)
        for side, w in enumerate((w_key, w_value)):
            first[o, side] = send(
                w.at[share_rows(target * part, quarter)],
                out_ref.at[head, share_rows(0, quarter), side * head_dim : (side + 1) * head_dim],
                send_sem.at[side, o - 1],
                z_sem.at[side, o - 1],
                head_peer(o),
            )
    local = []
    for at, (src, dst) in enumerate(((fresh, rows), (w_query, wq), (w_key, wk), (w_value, wv))):
        local.append(pltpu.make_async_copy(src, dst, load_sem.at[at]))
    for side, w in enumerate((w_key, w_value)):
        local.append(
            pltpu.make_async_copy(
                w.at[pl.ds(pl.multiple_of(head * part, 16), part)],
                out_ref.at[head, :, side * head_dim : (side + 1) * head_dim],
                own_sem.at[side],
            )
        )
    for copy in local:
        copy.start()
    for copy in local[:4]:
        copy.wait()

    def project(o):
        cut = slice(o * part, (o + 1) * part)
        left = rows[:, cut]
        for acc, w in ((q_acc, wq), (k_acc, wk), (v_acc, wv)):
            term = jnp.dot(left, w[cut, :], preferred_element_type=jnp.float32)
            if o == 0:
                acc[...] = term
            else:
                acc[...] += term

    project(0)
    for o in range(1, n_head):
        source = lax.rem(head + n_head - o, n_head)
        first[o, 0].wait_recv()
        first[o, 1].wait_recv()
        slot = out_ref.at[source, share_rows(0, quarter)]
        second[o] = send(slot, slot, send_sem.at[2, o - 1], x_sem.at[o - 1], x_mate)
        third[o] = send(slot, slot, send_sem.at[3, o - 1], c_sem.at[o - 1], c_mate)
        project(o)
    for o in range(1, n_head):
        source = lax.rem(head + n_head - o, n_head)
        second[o].wait_recv()
        slot = out_ref.at[source, share_rows(0, x_quarter)]
        fourth[o] = send(slot, slot, send_sem.at[4, o - 1], d_sem.at[o - 1], c_mate)

    def turn(raw, gain):
        mean_sq = jnp.mean(raw * raw, axis=-1, keepdims=True)
        normed = raw * lax.rsqrt(mean_sq + epsilon) * gain
        turned = pltpu.roll(normed, head_dim // 2, 1)
        return (normed * cos_ref[...] + turned * sin_ref[...]).astype(jnp.bfloat16)

    for j in range(q_acc.shape[1] // head_dim):
        cut = slice(j * head_dim, (j + 1) * head_dim)
        query_ref[:, cut] = turn(q_acc[:, cut], q_gain[...])
    new_key_ref[...] = turn(k_acc[...], k_gain[...])
    new_value_ref[...] = v_acc[...].astype(jnp.bfloat16)

    for o in range(1, n_head):
        third[o].wait_recv()
        fourth[o].wait_recv()
    for copy in sends:
        copy.wait_send()
    for copy in local[4:]:
        copy.wait()


def gather_weights(n_head, w_key, w_value, w_query, rows, q_gain, k_gain, cosine, sine):
    features, head_dim = w_key.shape
    new_count = rows.shape[0]
    bf16, f32 = jnp.bfloat16, jnp.float32
    any_space = pl.BlockSpec(memory_space=pl.ANY)
    vmem = pl.BlockSpec(memory_space=pltpu.VMEM)
    dma = pltpu.SemaphoreType.DMA
    return pl.pallas_call(
        functools.partial(weight_kernel, n_head),
        out_shape=(
            jax.ShapeDtypeStruct((n_head, features // n_head, 2 * head_dim), bf16),
            jax.ShapeDtypeStruct((new_count, w_query.shape[1]), bf16),
            jax.ShapeDtypeStruct((new_count, head_dim), bf16),
            jax.ShapeDtypeStruct((new_count, head_dim), bf16),
        ),
        in_specs=[any_space] * 4 + [vmem] * 4,
        out_specs=[any_space] + [vmem] * 3,
        scratch_shapes=[
            pltpu.VMEM(w_query.shape, bf16),
            pltpu.VMEM(w_key.shape, bf16),
            pltpu.VMEM(w_value.shape, bf16),
            pltpu.VMEM(rows.shape, bf16),
            pltpu.VMEM((new_count, w_query.shape[1]), f32),
            pltpu.VMEM((new_count, head_dim), f32),
            pltpu.VMEM((new_count, head_dim), f32),
            dma((2,)),
            dma((4,)),
            dma((5, n_head - 1)),
            dma((2, n_head - 1)),
            dma((n_head - 1,)),
            dma((n_head - 1,)),
            dma((n_head - 1,)),
        ],
        compiler_params=pltpu.CompilerParams(
            collective_id=0, has_side_effects=True, vmem_limit_bytes=48 * 1024 * 1024
        ),
        cost_estimate=pl.CostEstimate(
            flops=2 * rows.size * 768, bytes_accessed=16 << 20, transcendentals=0
        ),
    )(w_key, w_value, w_query, rows, q_gain[None, :], k_gain[None, :], cosine, sine)


def page_kernel(
    scale, n_block, session_ref, q_ref, gain_ref, page_turn, row_turn, *refs
):
    pair_refs = refs[:n_block]
    numer_ref, denom_ref, numer, denom = refs[n_block:]
    page_len, head_dim = row_turn.shape[1:]
    numer[...] = jnp.zeros_like(numer)
    denom[...] = jnp.zeros_like(denom)
    gain = gain_ref[...]

    for block, pair_ref in enumerate(pair_refs):
        pages = pair_ref.shape[0] // page_len

        def body(i, carry):
            p = block * pages + i
            s = session_ref[p]
            here = pl.ds(pl.multiple_of(i * page_len, 8), page_len)
            raw = pair_ref[here, :head_dim]
            mean_sq = jnp.mean(raw * raw, axis=-1, keepdims=True)
            normed = raw * lax.rsqrt(mean_sq + epsilon) * gain
            turned = pltpu.roll(normed, head_dim // 2, 1)
            page_cos, page_sin = page_turn[p, 0:1, :], page_turn[p, 1:2, :]
            cosine = page_cos * row_turn[0] - page_sin * row_turn[1]
            sine = page_sin * row_turn[2] + page_cos * row_turn[3]
            keys = (normed * cosine + turned * sine).astype(jnp.bfloat16)
            values = pair_ref[here, head_dim:].astype(jnp.bfloat16)
            scores = jnp.dot(keys, q_ref[s], preferred_element_type=jnp.float32)
            weight = jnp.exp(scores * scale)
            denom[s] += jnp.sum(weight.reshape(page_len // 8, 8, weight.shape[-1]), axis=0)
            numer[s] += lax.dot_general(
                values,
                weight.astype(jnp.bfloat16),
                (((0,), (0,)), ((), ())),
                preferred_element_type=jnp.float32,
            )
            return carry

        lax.fori_loop(0, pages, body, 0, unroll=2)
    numer_ref[...] = numer[...].astype(jnp.bfloat16)
    denom_ref[...] = denom[...]


def page_attention(session_of, queries, gain, page_turn, row_turn, pairs, scale):
    sess_count, head_dim, columns = queries.shape
    return pl.pallas_call(
        functools.partial(page_kernel, scale, len(pairs)),
        out_shape=(
            jax.ShapeDtypeStruct((sess_count, head_dim, columns), jnp.bfloat16),
            jax.ShapeDtypeStruct((sess_count, 8, columns), jnp.float32),
        ),
        in_specs=[pl.BlockSpec(memory_space=pltpu.SMEM)]
        + [pl.BlockSpec(memory_space=pltpu.VMEM)] * (4 + len(pairs)),
        out_specs=[pl.BlockSpec(memory_space=pltpu.VMEM)] * 2,
        scratch_shapes=[
            pltpu.VMEM((sess_count, head_dim, columns), jnp.float32),
            pltpu.VMEM((sess_count, 8, columns), jnp.float32),
        ],
        compiler_params=pltpu.CompilerParams(vmem_limit_bytes=48 * 1024 * 1024),
        cost_estimate=pl.CostEstimate(
            flops=4 * pairs[0].size * len(pairs) * columns // 2, bytes_accessed=6 << 20, transcendentals=0
        ),
    )(session_of, queries, gain[None, :], page_turn, row_turn, *pairs)


def shards(saved, fresh, w_query, w_key, w_value, q_gain, k_gain, lengths, slot_page):
    page_count, page_len, part_width = saved.shape
    head_dim = w_key.shape[1]
    n_head = lax.axis_size("head")
    n_store = lax.axis_size("store")
    my_store = lax.axis_index("store")
    sess_count = lengths.shape[0]
    head = lax.axis_index("head")
    head = lax.axis_index("head")
    half = head_dim // 2
    freqs = jnp.exp(
        -jnp.arange(half, dtype=jnp.float32) * (2.0 / head_dim) * math.log(rope_base)
    )
    turn_rows = fresh[0]
    new_count = turn_rows.shape[0]
    group_heads = w_query.shape[1] // head_dim
    my_length = lax.dynamic_index_in_dim(lengths, my_store, 0, keepdims=False)
    new_pos = my_length * page_len + jnp.arange(new_count, dtype=jnp.int32)
    angles = new_pos.astype(jnp.float32)[:, None] * freqs[None, :]
    new_cos, new_sin = jnp.cos(angles), jnp.sin(angles)
    w_here, queries, new_keys, new_values = gather_weights(
        n_head,
        w_key,
        w_value,
        w_query,
        turn_rows,
        q_gain,
        k_gain,
        jnp.concatenate([new_cos, new_cos], axis=-1),
        jnp.concatenate([-new_sin, new_sin], axis=-1),
    )
    w_here, slot_page, lengths = lax.optimization_barrier((w_here, slot_page, lengths))

    n_block = 3 if page_count % 3 == 0 else 1
    block_pages = page_count // n_block
    products = [
        (
            jnp.einsum(
                "rf,hfc->hrc",
                saved[i * block_pages : (i + 1) * block_pages].reshape(-1, part_width),
                w_here,
                preferred_element_type=jnp.float32,
            )
            * part_scale
        ).astype(jnp.float16)
        for i in range(n_block)
    ]

    def product(block, target):
        return lax.dynamic_index_in_dim(block, target, 0, keepdims=False).astype(jnp.float32)

    ups = [None] * n_block
    downs = [None] * n_block
    for r in range(n_head - 1):
        up_to = jnp.minimum(n_head - 1 - r + head, n_head - 1)
        down_to = jnp.maximum(r - (n_head - 1) + head, 0)
        up_pairs = [(i, i + 1) for i in range(r + 1)]
        down_pairs = [(n_head - 1 - i, n_head - 2 - i) for i in range(r + 1)]
        for i, block in enumerate(products):
            up = product(block, up_to)
            down = product(block, down_to)
            if r > 0:
                up = up + ups[i].astype(jnp.float32)
                down = down + downs[i].astype(jnp.float32)
            ups[i] = lax.ppermute(up.astype(jnp.float16), "head", up_pairs)
            downs[i] = lax.ppermute(down.astype(jnp.float16), "head", down_pairs)
    pairs = []
    for i, block in enumerate(products):
        total = product(block, head) + (
            ups[i].astype(jnp.float32) + downs[i].astype(jnp.float32)
        )
        pairs.append(total * (1.0 / part_scale))

    ends = jnp.cumsum(lengths)
    starts = ends - lengths
    session_of = jnp.sum((slot_page[:, None] >= ends[None, :]).astype(jnp.int32), axis=1)
    onehot = (session_of[:, None] == jnp.arange(sess_count, dtype=jnp.int32)[None, :]).astype(
        jnp.int32
    )
    first_page = jnp.sum(onehot * starts[None, :], axis=1)
    page_pos = (slot_page - first_page) * page_len
    page_angle = page_pos.astype(jnp.float32)[:, None] * freqs[None, :]
    page_turn = jnp.stack([jnp.cos(page_angle), jnp.sin(page_angle)], axis=1)
    page_turn = jnp.concatenate([page_turn, page_turn], axis=-1)
    row_angle = jnp.arange(page_len, dtype=jnp.float32)[:, None] * freqs[None, :]
    cosine, sine = jnp.cos(row_angle), jnp.sin(row_angle)
    row_turn = jnp.stack(
        [
            jnp.concatenate([cosine, cosine], axis=-1),
            jnp.concatenate([sine, sine], axis=-1),
            jnp.concatenate([-cosine, cosine], axis=-1),
            jnp.concatenate([-sine, sine], axis=-1),
        ]
    )

    scale = 1.0 / math.sqrt(head_dim)
    columns = group_heads * new_count
    q_t = (
        queries.reshape(new_count, group_heads, head_dim)
        .transpose(2, 1, 0)
        .reshape(head_dim, columns)
    )
    every_query = lax.all_gather(q_t, "store", axis=0)

    numer_t, denom_8 = page_attention(
        session_of, every_query, k_gain, page_turn, row_turn, pairs, scale
    )
    denom = jnp.sum(denom_8, axis=1)

    def packed(numer, denom):
        high = denom.astype(jnp.bfloat16)
        low = (denom - high.astype(jnp.float32)).astype(jnp.bfloat16)
        return jnp.concatenate(
            [numer.astype(jnp.bfloat16), high[:, None, :], low[:, None, :]], axis=1
        )

    core = lax.rem(my_store, 2)

    def of_core(array, c):
        cut = array.reshape((n_store // 2, 2) + array.shape[1:])
        return lax.dynamic_index_in_dim(cut, c, 1, keepdims=False)

    came = lax.ppermute(
        packed(of_core(numer_t, 1 - core), of_core(denom, 1 - core)),
        "store",
        [(i, i + 1 - 2 * (i % 2)) for i in range(n_store)],
    ).astype(jnp.float32)
    chip_numer = of_core(numer_t, core).astype(jnp.float32) + came[:, :head_dim]
    chip_denom = of_core(denom, core) + came[:, head_dim] + came[:, head_dim + 1]
    got = lax.all_to_all(
        packed(chip_numer, chip_denom),
        "store",
        0,
        0,
        tiled=True,
        axis_index_groups=[list(range(c, n_store, 2)) for c in range(2)],
    )
    total = jnp.sum(got.astype(jnp.float32), axis=0)

    own_scores = jnp.dot(new_keys, q_t, preferred_element_type=jnp.float32) * scale
    token = jnp.arange(columns, dtype=jnp.int32) % new_count
    causal = jnp.arange(new_count)[:, None] <= token[None, :]
    own_weight = jnp.where(causal, jnp.exp(own_scores), jnp.float32(0.0))
    own_denom = jnp.sum(own_weight, axis=0)
    own_numer = jnp.einsum(
        "kd,kc->dc", new_values, own_weight.astype(jnp.bfloat16), preferred_element_type=jnp.float32
    )
    numer = total[:head_dim] + own_numer
    denom = total[head_dim] + total[head_dim + 1] + own_denom
    attended = (numer / denom[None, :]).astype(jnp.bfloat16)
    attended = attended.reshape(head_dim, group_heads, new_count).transpose(2, 1, 0)
    return attended.reshape(1, new_count, group_heads * head_dim)


def solution(mesh):
    return jax.shard_map(
        shards,
        mesh=mesh,
        in_specs=(
            P(("group", "store"), None, "head"),
            P(("group", "store"), None, None),
            P(None, "head"),
            P(None, "head"),
            P(None, "head"),
            P(),
            P(),
            P("group"),
            P(("group", "store")),
        ),
        out_specs=P(("group", "store"), None, "head"),
        check_vma=False,
    )
```
